256 devices in a mesh: dp: 32 (over x, y, core), tensor: 8 (over z).
Axes of the slice: x: 4, y: 4, z: 8, core: 2. Of those that a mesh axis runs over, the one named last changes fastest.
Arguments:
- hidden: bfloat16 [12288, 14336], P('dp', 'tensor'), may hold values from -6 to 6
- destination: int32 [12288], P('dp'), may hold values from -1 to 12287, as said below
- job_per_tile: int32 [96], P('dp'), may hold values from 0 to 7
- down_matrix: bfloat16 [14336, 4096], P('tensor', 'dp'), may hold values from -0.046875 to 0.046875
- first_adapter_factors: bfloat16 [14336, 128], P('tensor'), may hold values from -0.046875 to 0.046875
- second_adapter_factors: bfloat16 [128, 4096], replicated, may hold values from -0.09375 to 0.09375
- cotangent: bfloat16 [12288, 4096], P(('dp', 'tensor')), may hold values from -6 to 6
Outputs:
- mixed: bfloat16 [12288, 4096], P(('dp', 'tensor'))
- packed_hidden_gradient: bfloat16 [12288, 14336], P('dp', 'tensor')
- grad_a: float32 [14336, 128], P('tensor')
- second_factor_gradient: float32 [128, 4096], replicated
The draws below stay inside these ranges and needn't reach their ends.
Inputs may be any that keep to these rules, and one draw needn't show every extreme that they name: `destination`: each loader row names the slot group * 384 + s of a data group, or -1 where no group takes it; no slot is named twice; the rows of one device name at most 12 slots of one group, and of every group some device names exactly 12; in every draw one group receives 12 rows from every device.
All inputs are finite; a program needn't handle non-finite values.
Results may differ from the reference program's by a relative error of at most 0.019.
Values may be sent and summed in bfloat16 or wider, within the bound.
No kernel may reach another device: no remote copies, remote signals or barrier semaphores. Data moves between devices by JAX's collectives and lax.ppermute only.
A program may use at most 128 MiB of HBM per device.

```python
import jax
import jax.numpy as jnp
from jax import lax

MODEL_DIM = 4096
HIDDEN_UNITS = 14336
ADAPTER_RANK = 16
ADAPTER_JOBS = 8
TILE = 128
TILES = 3
GROUP = 384
N_DP = 32
N_TENSOR = 8


def draw_destination(key, part):
    key = jax.random.fold_in(key, 11)
    subkeys = jax.random.split(key, 5)
    capacity = GROUP // N_DP
    sources = jnp.arange(N_DP, dtype=jnp.int32)
    counts = jax.random.randint(subkeys[0], (N_DP, N_DP), 0, capacity + 1).astype(jnp.int32)
    top_source = jax.random.randint(subkeys[1], (N_DP,), 0, N_DP).astype(jnp.int32)
    counts = jnp.where(sources[:, None] == top_source[None, :], capacity, counts)
    full_group = jax.random.randint(subkeys[2], (), 0, N_DP).astype(jnp.int32)
    counts = jnp.where(sources[None, :] == full_group, capacity, counts)
    slot_order = jax.vmap(lambda sub: jax.random.permutation(sub, GROUP))(jax.random.split(subkeys[3], N_DP)).astype(jnp.int32)
    row_order = jax.vmap(lambda sub: jax.random.permutation(sub, GROUP))(jax.random.split(subkeys[4], N_DP)).astype(jnp.int32)
    slot_start = jnp.cumsum(counts, axis=0) - counts
    row_start = jnp.cumsum(counts, axis=1) - counts
    offset = jnp.arange(capacity, dtype=jnp.int32)
    is_live = offset[None, None, :] < counts[:, :, None]
    slot_pos = jnp.clip(slot_start[:, :, None] + offset[None, None, :], 0, GROUP - 1)
    row_pos = jnp.clip(row_start[:, :, None] + offset[None, None, :], 0, GROUP - 1)
    slot_id = jnp.take_along_axis(jnp.broadcast_to(slot_order[None, :, :], (N_DP, N_DP, GROUP)), slot_pos, axis=2)
    row_id = jnp.take_along_axis(jnp.broadcast_to(row_order[:, None, :], (N_DP, N_DP, GROUP)), row_pos, axis=2)
    entries = jnp.where(is_live, sources[None, :, None] * GROUP + slot_id, -1).astype(jnp.int32)
    flat_row = jnp.where(is_live, sources[:, None, None] * GROUP + row_id, N_DP * GROUP).astype(jnp.int32)
    result = jnp.full((N_DP * GROUP + 1,), -1, jnp.int32).at[flat_row.reshape(-1)].set(entries.reshape(-1))
    return result[:N_DP * GROUP]


def set_ends(drawn, key, least, largest):
    longest = drawn.shape.index(max(drawn.shape))
    spots = []
    for shift in (0, 1):
        where = [jax.random.randint(jax.random.fold_in(key, axis), (), 0, length) for axis, length in enumerate(drawn.shape)]
        where[longest] = (where[longest] + shift) % drawn.shape[longest]
        spots.append(tuple(where))
    return drawn.at[spots[0]].set(least).at[spots[1]].set(largest)


def levels(stream_key, shape, pieces, low, largest):
    level = 1.0
    for dim, shards_of in pieces:
        steps = jax.random.uniform(jax.random.fold_in(jax.random.fold_in(stream_key, 6), dim), (shards_of,), jnp.float32, low / len(pieces), largest / len(pieces))
        level = level * jnp.repeat(jnp.exp(steps), shape[dim] // shards_of).reshape((-1,) + (1,) * (len(shape) - 1 - dim))
    return level


def noise(own_key, extent, spread, bound, shards=(), kind=jnp.bfloat16):
    level = levels(own_key, extent, shards, -0.22, 0.18) if shards else 1.0
    drawn = jax.random.normal(own_key, extent, jnp.float32) * spread * level
    return jnp.minimum(jnp.maximum(drawn, -bound), bound).astype(kind)


def setup_inputs(seed: int = 0) -> dict:
    seeds = jax.random.split(jax.random.key(seed), 8)
    hidden = noise(seeds[0], (N_DP * GROUP, HIDDEN_UNITS), 1.0, 6.0, ((0, 32), (1, 8)))
    destination = draw_destination(jax.random.fold_in(seeds[7], 71), 0)
    job_per_tile = set_ends(jax.random.randint(seeds[2], (N_DP * TILES,), 0, ADAPTER_JOBS), jax.random.fold_in(seeds[2], 1), 0, ADAPTER_JOBS - 1).astype(jnp.int32)
    down_matrix = noise(seeds[3], (HIDDEN_UNITS, MODEL_DIM), HIDDEN_UNITS ** -0.5, 0.046875, ((0, 8), (1, 32)))
    first_adapter_factors = noise(seeds[4], (HIDDEN_UNITS, ADAPTER_JOBS * ADAPTER_RANK), HIDDEN_UNITS ** -0.5, 0.046875, ((0, 8),))
    second_adapter_factors = noise(seeds[5], (ADAPTER_JOBS * ADAPTER_RANK, MODEL_DIM), MODEL_DIM ** -0.5, 0.09375)
    cotangent = noise(seeds[6], (N_DP * GROUP, MODEL_DIM), 0.5, 6.0, ((0, 256),))
    return {"hidden": hidden, "destination": destination, "job_per_tile": job_per_tile, "down_matrix": down_matrix, "first_adapter_factors": first_adapter_factors, "second_adapter_factors": second_adapter_factors, "cotangent": cotangent}


adapter_scale = 2.0


def rounded(values):
    return lax.optimization_barrier(values.astype(jnp.bfloat16)).astype(jnp.float32)


def contract_trailing(left, right):
    return lax.dot_general(left, right, (((1,), (1,)), ((), ())), preferred_element_type=jnp.float32)


def contract_leading(left, right):
    return lax.dot_general(left, right, (((0,), (0,)), ((), ())), preferred_element_type=jnp.float32)


def reference(hidden, destination, job_per_tile, down_matrix, first_adapter_factors, second_adapter_factors, cotangent):
    slot_total = N_DP * GROUP
    hidden_unit_count = HIDDEN_UNITS // N_TENSOR
    target = jnp.where(destination >= 0, destination, slot_total).astype(jnp.int32)
    packed_hidden = jnp.zeros((slot_total + 1, HIDDEN_UNITS), hidden.dtype).at[target].set(hidden)[:slot_total]
    slot_job = job_per_tile[jnp.arange(slot_total, dtype=jnp.int32) // TILE]
    job_of_column = jnp.arange(ADAPTER_JOBS * ADAPTER_RANK, dtype=jnp.int32) // ADAPTER_RANK
    job_selector = slot_job[:, None] == job_of_column[None, :]

    def accumulate(running, block_index):
        base_sum, inner_sum = running
        block_offset = (block_index * hidden_unit_count).astype(jnp.int32)
        rows_part = lax.dynamic_slice_in_dim(packed_hidden, block_offset, hidden_unit_count, 1)
        weight_part = lax.dynamic_slice_in_dim(down_matrix, block_offset, hidden_unit_count, 0)
        factor_portion = lax.dynamic_slice_in_dim(first_adapter_factors, block_offset, hidden_unit_count, 0)
        base_term = jnp.dot(rows_part, weight_part, preferred_element_type=jnp.float32)
        inner_term = jnp.where(job_selector, jnp.dot(rows_part, factor_portion, preferred_element_type=jnp.float32), 0.0)
        return (base_sum + rounded(base_term), inner_sum + rounded(inner_term)), None

    start_values = (jnp.zeros((slot_total, MODEL_DIM), jnp.float32), jnp.zeros((slot_total, ADAPTER_JOBS * ADAPTER_RANK), jnp.float32))
    (base_output, inner), unused = lax.scan(accumulate, start_values, jnp.arange(N_TENSOR, dtype=jnp.int32))
    inner_truncated = inner.astype(jnp.bfloat16)
    mixed = (base_output + adapter_scale * jnp.dot(inner_truncated, second_adapter_factors, preferred_element_type=jnp.float32)).astype(jnp.bfloat16)
    inner_gradient = jnp.where(job_selector, adapter_scale * contract_trailing(cotangent, second_adapter_factors), 0.0).astype(jnp.bfloat16)

    def grad_block(block_index):
        block_offset = (block_index * hidden_unit_count).astype(jnp.int32)
        weight_part = lax.dynamic_slice_in_dim(down_matrix, block_offset, hidden_unit_count, 0)
        factor_portion = lax.dynamic_slice_in_dim(first_adapter_factors, block_offset, hidden_unit_count, 0)
        backward = contract_trailing(cotangent, weight_part) + contract_trailing(inner_gradient, factor_portion)
        return backward.astype(jnp.bfloat16)

    blocks = lax.map(grad_block, jnp.arange(N_TENSOR, dtype=jnp.int32))
    packed_hidden_gradient = jnp.transpose(blocks, (1, 0, 2)).reshape(slot_total, HIDDEN_UNITS)
    grad_a = contract_leading(packed_hidden, inner_gradient)
    second_factor_gradient = adapter_scale * contract_leading(inner_truncated, cotangent)
    return (mixed, packed_hidden_gradient, grad_a, second_factor_gradient)
```

```python
import functools

import jax
import jax.numpy as jnp
from jax import lax
from jax.experimental import pallas as pl
from jax.experimental.pallas import tpu as pltpu
from jax.sharding import PartitionSpec as P

ADAPTER_RANK = 16
ADAPTER_SCALE = 2.0
NX, NY, NZ = 4, 4, 8
CHIPS = NX * NY
LANES = 128
VMEM_LIMIT = 40 * 1024 * 1024
F32 = jnp.float32
BF16 = jnp.bfloat16

SAME_CORE = [[2 * chip + core for chip in range(CHIPS)] for core in range(2)]


def after(values, *others):
    return lax.optimization_barrier((values, others))[0]


def swap_core(value):
    return lax.ppermute(value, "dp", [(i, i ^ 1) for i in range(2 * CHIPS)])


def dot_nt(left, right):
    return lax.dot_general(left, right, (((1,), (1,)), ((), ())), preferred_element_type=F32)


def dot_nn(left, right):
    return jnp.dot(left, right, preferred_element_type=F32)


def dot_tn(left, right):
    return lax.dot_general(left, right, (((0,), (0,)), ((), ())), preferred_element_type=F32)


def params(limit=VMEM_LIMIT):
    return pltpu.CompilerParams(vmem_limit_bytes=limit)


VM = pl.BlockSpec(memory_space=pltpu.VMEM)
SM = pl.BlockSpec(memory_space=pltpu.SMEM)


def sort_kernel(dest_ref, hidden_ref, out_ref):
    rows, units = hidden_ref.shape
    capacity = rows // (2 * CHIPS)
    dest = dest_ref[...]
    live = dest >= 0
    dest_f = dest.astype(F32)
    group = jnp.where(live, jnp.floor((dest_f + 0.5) * (1.0 / rows)), -1.0)
    across = jnp.broadcast_to(group, (rows, rows))
    down = across.T
    sub = lax.broadcasted_iota(jnp.int32, (rows, rows), 0)
    lane = lax.broadcasted_iota(jnp.int32, (rows, rows), 1)
    earlier = jnp.where((across == down) & (sub < lane), 1.0, 0.0)
    position = jnp.sum(earlier, axis=0, keepdims=True)
    place = jnp.where(live, group * capacity + position, -1.0)
    pick = jnp.where(sub.astype(F32) == place, 1.0, 0.0).astype(BF16)
    for tile in range(units // 256):
        cols = slice(tile * 256, (tile + 1) * 256)
        out_ref[:, cols] = dot_nn(pick, hidden_ref[:, cols]).astype(BF16)
    chip = jnp.floor((dest_f + 0.5) * (1.0 / (2 * rows)))
    code = jnp.where(live, dest_f - chip * (2 * rows) + 1.0, 0.0)
    high = jnp.floor(code * (1.0 / 16.0))
    low = code - 16.0 * high
    row = lax.broadcasted_iota(jnp.int32, (LANES, rows), 0)
    codes = jnp.where(row == 0, high, jnp.where(row == 1, low, 0.0)).astype(BF16)
    out_ref[:, units:] = dot_nt(pick, codes).astype(BF16)


def sort_rows(destination, hidden):
    rows, units = hidden.shape
    return pl.pallas_call(
        sort_kernel,
        out_shape=jax.ShapeDtypeStruct((rows, units + LANES), BF16),
        in_specs=[VM, VM],
        out_specs=VM,
        compiler_params=params(),
    )(destination.reshape(1, rows), hidden)


def pack_kernel(core_ref, mine_ref, other_ref, out_ref):
    slots, units = out_ref.shape
    rows = mine_ref.shape[0]
    weight_row = lax.broadcasted_iota(jnp.int32, (8, LANES), 1)
    weight = jnp.where(weight_row == 0, 16.0, jnp.where(weight_row == 1, 1.0, 0.0)).astype(BF16)
    wanted = lax.broadcasted_iota(jnp.int32, (slots, rows), 0) + core_ref[0] * slots + 1
    wanted = wanted.astype(F32)
    picks = []
    for got in (mine_ref, other_ref):
        code = dot_nt(weight, got[:, units:])[0:1, :]
        picks.append(jnp.where(wanted == code, 1.0, 0.0).astype(BF16))
    for tile in range(units // 256):
        cols = slice(tile * 256, (tile + 1) * 256)
        out_ref[:, cols] = (
            dot_nn(picks[0], mine_ref[:, cols]) + dot_nn(picks[1], other_ref[:, cols])
        ).astype(BF16)


def pack_rows(core, mine, other):
    rows, wide = mine.shape
    return pl.pallas_call(
        pack_kernel,
        out_shape=jax.ShapeDtypeStruct((rows, wide - LANES), BF16),
        in_specs=[SM, VM, VM],
        out_specs=VM,
        compiler_params=params(),
    )(core.reshape(1), mine, other)


def cotangent_kernel(z_ref, jobs_ref, cot_ref, second_ref, out_ref):
    rows, model = cot_ref.shape
    inner = ADAPTER_SCALE * dot_nt(cot_ref[...], second_ref[...])
    width = inner.shape[1]
    slot = lax.broadcasted_iota(jnp.int32, (rows, width), 0) + z_ref[0] * rows
    tile = NZ * rows // 3
    job = jnp.where(slot < tile, jobs_ref[0], jnp.where(slot < 2 * tile, jobs_ref[1], jobs_ref[2]))
    column = lax.broadcasted_iota(jnp.int32, (rows, width), 1)
    first = job * ADAPTER_RANK
    chosen = (column >= first) & (column < first + ADAPTER_RANK)
    out_ref[:, :model] = cot_ref[...]
    out_ref[:, model:] = jnp.where(chosen, inner, 0.0).astype(BF16)


def widen_cotangent(z, jobs, cotangent, second):
    rows, model = cotangent.shape
    return pl.pallas_call(
        cotangent_kernel,
        out_shape=jax.ShapeDtypeStruct((rows, model + second.shape[0]), BF16),
        in_specs=[SM, SM, VM, VM],
        out_specs=VM,
        compiler_params=params(),
    )(z.reshape(1), jobs, cotangent, second)


def order_kernel(half, z_ref, *refs):
    pieces, (model_ref, inner_ref, sem) = refs[:-3], refs[-3:]
    model = model_ref.shape[2]
    copies = []

    def copy(source, out_ref, offset, start, size):
        spot = lax.rem(z_ref[0] + (offset + NZ), NZ)
        copies.append(
            pltpu.make_async_copy(
                source, out_ref.at[spot, :, pl.ds(start, size)], sem.at[len(copies)]
            )
        )
        copies[-1].start()

    for piece, offset in zip(pieces[:-2], range(1 - NZ // 2, NZ // 2)):
        copy(piece.at[:, pl.ds(0, model)], model_ref, offset, 0, model)
        copy(piece.at[:, pl.ds(model, LANES)], inner_ref, offset, 0, LANES)
    low, high = pieces[-2:]
    copy(low, model_ref, NZ // 2, 0, half)
    copy(high.at[:, pl.ds(0, model - half)], model_ref, NZ // 2, half, model - half)
    copy(high.at[:, pl.ds(model - half, LANES)], inner_ref, NZ // 2, 0, LANES)
    for started in copies:
        started.wait()


def send_z(value, step):
    return lax.ppermute(value, "tensor", [(i, (i + step) % NZ) for i in range(NZ)])


def gather_z(piece, z):
    rows, wide = piece.shape
    half = wide // (2 * LANES) * LANES
    up = down = piece
    pieces = [piece]
    for step in range(1, NZ // 2):
        up, down = lax.optimization_barrier((send_z(up, 1), send_z(down, -1)))
        pieces = [up] + pieces + [down]
        if step == 2:
            between = (up, down)
    pieces += lax.optimization_barrier((send_z(up[:, :half], 1), send_z(down[:, half:], -1)))
    anywhere = pl.BlockSpec(memory_space=pl.ANY)
    model, inner = pl.pallas_call(
        functools.partial(order_kernel, half),
        out_shape=(
            jax.ShapeDtypeStruct((NZ, rows, wide - LANES), BF16),
            jax.ShapeDtypeStruct((NZ, rows, LANES), BF16),
        ),
        in_specs=[SM] + [anywhere] * len(pieces),
        out_specs=(VM, VM),
        scratch_shapes=[pltpu.SemaphoreType.DMA((2 * NZ + 1,))],
        compiler_params=params(),
    )(z.reshape(1), *pieces)
    return model.reshape(NZ * rows, -1), inner.reshape(NZ * rows, LANES), between


def sum_z(value):
    step = 1
    while step < NZ:
        value = value + lax.ppermute(value, "tensor", [(i, i ^ step) for i in range(NZ)])
        step *= 2
    return value


def gather_xor(value):
    step = 1
    while step < NZ:
        other = lax.ppermute(value, "tensor", [(i, i ^ step) for i in range(NZ)])
        value = jnp.concatenate([value, other], axis=0)
        step *= 2
    return value


def share_kernel(z_ref, inner_ref, cot_ref, first_ref, out_ref):
    parts, rows, _ = out_ref.shape
    firsts = first_ref.shape[0] // parts
    seconds = rows - firsts
    wide = cot_ref.shape[1] // NZ
    column = pl.multiple_of(z_ref[0] * wide, LANES)
    block = ADAPTER_SCALE * dot_nn(inner_ref[...], cot_ref[:, pl.ds(column, wide)])
    block = block.astype(BF16)
    each = block.shape[0] // seconds
    for i in range(parts):
        out_ref[i, :firsts, :] = first_ref[i * firsts : (i + 1) * firsts, :]
        row, column = (i % each) * seconds, (i // each) * LANES
        out_ref[i, firsts:, :] = block[row : row + seconds, column : column + LANES]


def shares(z, inner, cotangent, first_part):
    parts = 2 * CHIPS
    rows = first_part.shape[0] // parts + inner.shape[0] * cotangent.shape[1] // (NZ * parts * LANES)
    return pl.pallas_call(
        share_kernel,
        out_shape=jax.ShapeDtypeStruct((parts, rows, LANES), BF16),
        in_specs=[SM, VM, VM, VM],
        out_specs=VM,
        compiler_params=params(),
    )(z.reshape(1), inner, cotangent, first_part)


def finish_kernel(z_ref, every_ref, first_ref, second_ref):
    parts, rows, _ = every_ref.shape
    firsts = first_ref.shape[0] // parts
    seconds = (rows - firsts) // NZ
    each = second_ref.shape[0] // seconds
    wide = second_ref.shape[1] // NZ
    for i in range(parts):
        first_ref[i * firsts : (i + 1) * firsts, :] = every_ref[i, :firsts, :].astype(F32)
        share = every_ref[i, firsts:, :].astype(F32)
        row = (i % each) * seconds
        for place in range(NZ):
            column = (z_ref[0] ^ place) * wide + (i // each) * LANES
            second_ref[row : row + seconds, pl.ds(pl.multiple_of(column, LANES), LANES)] = share[
                place * seconds : (place + 1) * seconds
            ]


def finish(z, every, units, width, model):
    return pl.pallas_call(
        finish_kernel,
        out_shape=(
            jax.ShapeDtypeStruct((units, width), F32),
            jax.ShapeDtypeStruct((width, model), F32),
        ),
        in_specs=[SM, VM],
        out_specs=(VM, VM),
        compiler_params=params(),
    )(z.reshape(1), every)


def forward_kernel(packed_ref, weight_ref, out_ref):
    out_ref[...] = dot_nt(packed_ref[...], weight_ref[...]).astype(BF16)


def forward(packed, weight):
    (slots, units), model = packed.shape, weight.shape[0]
    tile = 1024
    return pl.pallas_call(
        forward_kernel,
        grid=(model // tile,),
        out_shape=jax.ShapeDtypeStruct((slots, model), BF16),
        in_specs=[
            pl.BlockSpec((slots, units), lambda i: (0, 0)),
            pl.BlockSpec((tile, units), lambda i: (i, 0)),
        ],
        out_specs=pl.BlockSpec((slots, tile), lambda i: (0, i)),
        compiler_params=params(),
        cost_estimate=pl.CostEstimate(
            flops=2 * slots * units * model,
            bytes_accessed=2 * (slots * units + units * model + slots * model),
            transcendentals=0,
        ),
    )(packed, weight)


def backward_kernel(cot_ref, inner_ref, weight_ref, first_ref, out_ref):
    total = dot_nn(cot_ref[...], weight_ref[...]) + dot_nt(inner_ref[...], first_ref[...])
    out_ref[...] = total.astype(BF16)


def backward(cotangent, inner_gradient, weight, first_factors):
    (slots, model), units = cotangent.shape, weight.shape[1]
    tile = 896
    return pl.pallas_call(
        backward_kernel,
        grid=(units // tile,),
        out_shape=jax.ShapeDtypeStruct((slots, units), BF16),
        in_specs=[
            pl.BlockSpec((slots, model), lambda i: (0, 0)),
            pl.BlockSpec((slots, LANES), lambda i: (0, 0)),
            pl.BlockSpec((model, tile), lambda i: (0, i)),
            pl.BlockSpec((tile, LANES), lambda i: (i, 0)),
        ],
        out_specs=pl.BlockSpec((slots, tile), lambda i: (0, i)),
        compiler_params=params(),
        cost_estimate=pl.CostEstimate(
            flops=2 * slots * units * model,
            bytes_accessed=2 * (slots * units + units * model + slots * model),
            transcendentals=0,
        ),
    )(cotangent, inner_gradient, weight, first_factors)


def on_device(hidden, destination, job_per_tile, down_matrix, first_factors, second_factors, cotangent):
    rows, units = hidden.shape
    shard = rows // NZ
    width, model = second_factors.shape
    core = lax.rem(lax.axis_index("dp"), 2)
    z = lax.axis_index("tensor")

    weight = lax.all_gather(down_matrix.T, "dp", axis=0, tiled=True)
    sent = sort_rows(destination, hidden)
    got = lax.all_to_all(
        sent, "dp", split_axis=0, concat_axis=0, axis_index_groups=SAME_CORE, tiled=True
    )
    piece = widen_cotangent(z, job_per_tile, cotangent, second_factors)
    full_cotangent, inner_gradient, between = gather_z(piece, z)
    got = after(got, *between)

    packed = pack_rows(core, got, swap_core(got))
    slot_job = jnp.repeat(job_per_tile, rows // job_per_tile.shape[0], total_repeat_length=rows)
    column = jnp.arange(width, dtype=jnp.int32)
    column_job = column // ADAPTER_RANK
    inner_part = jnp.where(
        slot_job[:, None] == column_job[None, :], dot_nn(packed, first_factors), 0.0
    ).astype(BF16)
    fold = (column[None, :] % ADAPTER_RANK == jnp.arange(ADAPTER_RANK)[:, None]).astype(BF16)
    inner_sum = sum_z(dot_nt(fold, inner_part)).astype(BF16)
    inner = jnp.where(
        slot_job[None, :] == column_job[:, None], jnp.tile(inner_sum, (width // ADAPTER_RANK, 1)), 0
    ).astype(BF16)
    my_slots = (
        jnp.arange(rows, dtype=jnp.int32)[:, None]
        == z * shard + jnp.arange(shard, dtype=jnp.int32)[None, :]
    ).astype(BF16)
    my_inner = lax.dot_general(
        my_slots, inner, (((0,), (1,)), ((), ())), preferred_element_type=F32
    ).astype(BF16)

    first_part = dot_tn(packed, inner_gradient).astype(BF16)
    sums = shares(z, inner, full_cotangent, first_part)
    parts = lax.all_to_all(sums, "dp", split_axis=0, concat_axis=0, tiled=True)
    share = jnp.sum(parts.astype(F32), axis=0).astype(BF16)
    firsts = units // (2 * CHIPS)
    share = jnp.concatenate([share[:firsts], gather_xor(share[firsts:])], axis=0)
    spread = jnp.broadcast_to(share[None], (2 * CHIPS,) + share.shape)
    every = lax.all_to_all(spread, "dp", split_axis=0, concat_axis=0, tiled=True)

    weight = after(weight, sums)
    base = after(forward(packed, weight), parts)
    summed = lax.psum_scatter(base, "tensor", scatter_dimension=0, tiled=True)
    hidden_gradient = backward(full_cotangent, inner_gradient, weight, first_factors)
    grad_a, second_gradient = finish(z, after(every, hidden_gradient), units, width, model)
    mixed = (
        summed.astype(F32) + ADAPTER_SCALE * dot_nn(my_inner, second_factors)
    ).astype(BF16)
    return (mixed, hidden_gradient, grad_a, second_gradient)


def solution(mesh):
    return jax.shard_map(
        on_device,
        mesh=mesh,
        in_specs=(
            P("dp", "tensor"),
            P("dp"),
            P("dp"),
            P("tensor", "dp"),
            P("tensor", None),
            P(),
            P(("dp", "tensor"), None),
        ),
        out_specs=(P(("dp", "tensor"), None), P("dp", "tensor"), P("tensor", None), P()),
        check_vma=False,
    )
```

```python
import functools

import jax
import jax.numpy as jnp
from jax import lax
from jax.experimental import pallas as pl
from jax.experimental.pallas import tpu as pltpu
from jax.sharding import PartitionSpec as P

ADAPTER_RANK = 16
ADAPTER_SCALE = 2.0
NX, NY, NZ = 4, 4, 8
CHIPS = NX * NY
LANES = 128
VMEM_LIMIT = 40 * 1024 * 1024
WHOLE_VMEM = 58 * 1024 * 1024
F32 = jnp.float32
BF16 = jnp.bfloat16

SAME_CORE = [[2 * chip + core for chip in range(CHIPS)] for core in range(2)]


def after(values, *others):
    return lax.optimization_barrier((values, others))[0]


def swap_core(value):
    return lax.ppermute(value, "dp", [(i, i ^ 1) for i in range(2 * CHIPS)])


def dot_nt(left, right):
    return lax.dot_general(left, right, (((1,), (1,)), ((), ())), preferred_element_type=F32)


def dot_nn(left, right):
    return jnp.dot(left, right, preferred_element_type=F32)


def dot_tn(left, right):
    return lax.dot_general(left, right, (((0,), (0,)), ((), ())), preferred_element_type=F32)


def params(limit=VMEM_LIMIT):
    return pltpu.CompilerParams(vmem_limit_bytes=limit)


VM = pl.BlockSpec(memory_space=pltpu.VMEM)
SM = pl.BlockSpec(memory_space=pltpu.SMEM)


def sort_kernel(dest_ref, hidden_ref, out_ref):
    rows, units = hidden_ref.shape
    capacity = rows // (2 * CHIPS)
    dest = dest_ref[...]
    live = dest >= 0
    dest_f = dest.astype(F32)
    group = jnp.where(live, jnp.floor((dest_f + 0.5) * (1.0 / rows)), -1.0)
    across = jnp.broadcast_to(group, (rows, rows))
    down = across.T
    sub = lax.broadcasted_iota(jnp.int32, (rows, rows), 0)
    lane = lax.broadcasted_iota(jnp.int32, (rows, rows), 1)
    earlier = jnp.where((across == down) & (sub < lane), 1.0, 0.0)
    position = jnp.sum(earlier, axis=0, keepdims=True)
    place = jnp.where(live, group * capacity + position, -1.0)
    pick = jnp.where(sub.astype(F32) == place, 1.0, 0.0).astype(BF16)
    for tile in range(units // 256):
        cols = slice(tile * 256, (tile + 1) * 256)
        out_ref[:, cols] = dot_nn(pick, hidden_ref[:, cols]).astype(BF16)
    chip = jnp.floor((dest_f + 0.5) * (1.0 / (2 * rows)))
    code = jnp.where(live, dest_f - chip * (2 * rows) + 1.0, 0.0)
    high = jnp.floor(code * (1.0 / 16.0))
    low = code - 16.0 * high
    row = lax.broadcasted_iota(jnp.int32, (LANES, rows), 0)
    codes = jnp.where(row == 0, high, jnp.where(row == 1, low, 0.0)).astype(BF16)
    out_ref[:, units:] = dot_nt(pick, codes).astype(BF16)


def sort_rows(destination, hidden):
    rows, units = hidden.shape
    return pl.pallas_call(
        sort_kernel,
        out_shape=jax.ShapeDtypeStruct((rows, units + LANES), BF16),
        in_specs=[VM, VM],
        out_specs=VM,
        compiler_params=params(),
    )(destination.reshape(1, rows), hidden)


def pack_kernel(core_ref, mine_ref, other_ref, out_ref):
    slots, units = out_ref.shape
    rows = mine_ref.shape[0]
    weight_row = lax.broadcasted_iota(jnp.int32, (8, LANES), 1)
    weight = jnp.where(weight_row == 0, 16.0, jnp.where(weight_row == 1, 1.0, 0.0)).astype(BF16)
    wanted = lax.broadcasted_iota(jnp.int32, (slots, rows), 0) + core_ref[0] * slots + 1
    wanted = wanted.astype(F32)
    picks = []
    for got in (mine_ref, other_ref):
        code = dot_nt(weight, got[:, units:])[0:1, :]
        picks.append(jnp.where(wanted == code, 1.0, 0.0).astype(BF16))
    for tile in range(units // 256):
        cols = slice(tile * 256, (tile + 1) * 256)
        out_ref[:, cols] = (
            dot_nn(picks[0], mine_ref[:, cols]) + dot_nn(picks[1], other_ref[:, cols])
        ).astype(BF16)


def pack_rows(core, mine, other):
    rows, wide = mine.shape
    return pl.pallas_call(
        pack_kernel,
        out_shape=jax.ShapeDtypeStruct((rows, wide - LANES), BF16),
        in_specs=[SM, VM, VM],
        out_specs=VM,
        compiler_params=params(),
    )(core.reshape(1), mine, other)


def cotangent_kernel(z_ref, jobs_ref, cot_ref, second_ref, out_ref):
    rows, model = cot_ref.shape
    inner = ADAPTER_SCALE * dot_nt(cot_ref[...], second_ref[...])
    width = inner.shape[1]
    slot = lax.broadcasted_iota(jnp.int32, (rows, width), 0) + z_ref[0] * rows
    tile = NZ * rows // 3
    job = jnp.where(slot < tile, jobs_ref[0], jnp.where(slot < 2 * tile, jobs_ref[1], jobs_ref[2]))
    column = lax.broadcasted_iota(jnp.int32, (rows, width), 1)
    first = job * ADAPTER_RANK
    chosen = (column >= first) & (column < first + ADAPTER_RANK)
    out_ref[:, :model] = cot_ref[...]
    out_ref[:, model:] = jnp.where(chosen, inner, 0.0).astype(BF16)


def widen_cotangent(z, jobs, cotangent, second):
    rows, model = cotangent.shape
    return pl.pallas_call(
        cotangent_kernel,
        out_shape=jax.ShapeDtypeStruct((rows, model + second.shape[0]), BF16),
        in_specs=[SM, SM, VM, VM],
        out_specs=VM,
        compiler_params=params(),
    )(z.reshape(1), jobs, cotangent, second)


def order_kernel(half, z_ref, *refs):
    pieces, (model_ref, inner_ref, sem) = refs[:-3], refs[-3:]
    model = model_ref.shape[2]
    copies = []

    def copy(source, out_ref, offset, start, size):
        spot = lax.rem(z_ref[0] + (offset + NZ), NZ)
        copies.append(
            pltpu.make_async_copy(
                source, out_ref.at[spot, :, pl.ds(start, size)], sem.at[len(copies)]
            )
        )
        copies[-1].start()

    for piece, offset in zip(pieces[:-2], range(1 - NZ // 2, NZ // 2)):
        copy(piece.at[:, pl.ds(0, model)], model_ref, offset, 0, model)
        copy(piece.at[:, pl.ds(model, LANES)], inner_ref, offset, 0, LANES)
    low, high = pieces[-2:]
    copy(low, model_ref, NZ // 2, 0, half)
    copy(high.at[:, pl.ds(0, model - half)], model_ref, NZ // 2, half, model - half)
    copy(high.at[:, pl.ds(model - half, LANES)], inner_ref, NZ // 2, 0, LANES)
    for started in copies:
        started.wait()


def send_z(value, step):
    return lax.ppermute(value, "tensor", [(i, (i + step) % NZ) for i in range(NZ)])


def gather_near(piece):
    steps, up, down = [], piece, piece
    for _ in range(1, NZ // 2):
        up, down = lax.optimization_barrier((send_z(up, 1), send_z(down, -1)))
        steps.append((up, down))
    return steps


def gather_far(piece, steps, last, z):
    rows, wide = piece.shape
    half = wide // (2 * LANES) * LANES
    up, down = last
    far = lax.optimization_barrier((send_z(up[:, :half], 1), send_z(down[:, half:], -1)))
    pieces = [up for up, _ in steps[::-1]] + [piece] + [down for _, down in steps] + list(far)
    anywhere = pl.BlockSpec(memory_space=pl.ANY)
    model, inner = pl.pallas_call(
        functools.partial(order_kernel, half),
        out_shape=(
            jax.ShapeDtypeStruct((NZ, rows, wide - LANES), BF16),
            jax.ShapeDtypeStruct((NZ, rows, LANES), BF16),
        ),
        in_specs=[SM] + [anywhere] * len(pieces),
        out_specs=(VM, VM),
        scratch_shapes=[pltpu.SemaphoreType.DMA((2 * NZ + 1,))],
        compiler_params=params(),
    )(z.reshape(1), *pieces)
    return model.reshape(NZ * rows, -1), inner.reshape(NZ * rows, LANES)


def sum_z(value):
    step = 1
    while step < NZ:
        value = value + lax.ppermute(value, "tensor", [(i, i ^ step) for i in range(NZ)])
        step *= 2
    return value


def gather_xor(value):
    step = 1
    while step < NZ:
        other = lax.ppermute(value, "tensor", [(i, i ^ step) for i in range(NZ)])
        value = jnp.concatenate([value, other], axis=0)
        step *= 2
    return value


def share_kernel(_, inner_ref, cot_ref, first_ref, out_ref):
    parts, rows, _ = out_ref.shape
    firsts = first_ref.shape[0] // parts
    seconds = rows - firsts
    block = (ADAPTER_SCALE * dot_nn(inner_ref[...], cot_ref[...])).astype(BF16)
    each = block.shape[0] // seconds
    for i in range(parts):
        out_ref[i, :firsts, :] = first_ref[i * firsts : (i + 1) * firsts, :]
        row, column = (i % each) * seconds, (i // each) * LANES
        out_ref[i, firsts:, :] = block[row : row + seconds, column : column + LANES]


def shares(z, inner, cotangent, first_part):
    parts = 2 * CHIPS
    rows = first_part.shape[0] // parts + inner.shape[0] * cotangent.shape[1] // (NZ * parts * LANES)
    slots, model = cotangent.shape
    return pl.pallas_call(
        share_kernel,
        out_shape=jax.ShapeDtypeStruct((parts, rows, LANES), BF16),
        grid_spec=pltpu.PrefetchScalarGridSpec(
            num_scalar_prefetch=1,
            grid=(1,),
            in_specs=[
                pl.BlockSpec(inner.shape, lambda i, z: (0, 0)),
                pl.BlockSpec((slots, model // NZ), lambda i, z: (0, z[0])),
                pl.BlockSpec(first_part.shape, lambda i, z: (0, 0)),
            ],
            out_specs=pl.BlockSpec((parts, rows, LANES), lambda i, z: (0, 0, 0)),
        ),
        compiler_params=params(WHOLE_VMEM),
    )(z.reshape(1), inner, cotangent, first_part)


def finish_kernel(place_ref, mine_ref, other_ref, first_ref, second_ref):
    chips, rows, _ = mine_ref.shape
    firsts = first_ref.shape[0] // (2 * chips)
    seconds = (rows - firsts) // NZ
    each = second_ref.shape[0] // seconds
    wide = second_ref.shape[1] // NZ
    for core, part_ref in ((place_ref[1], mine_ref), (1 - place_ref[1], other_ref)):
        for chip in range(chips):
            spot = pl.multiple_of((2 * chip + core) * firsts, 8)
            first_ref[pl.ds(spot, firsts), :] = part_ref[chip, :firsts, :].astype(F32)
            share = part_ref[chip, firsts:, :].astype(F32)
            row = pl.multiple_of(((2 * chip) % each + core) * seconds, 8)
            for place in range(NZ):
                column = (place_ref[0] ^ place) * wide + (2 * chip // each) * LANES
                second_ref[pl.ds(row, seconds), pl.ds(pl.multiple_of(column, LANES), LANES)] = share[
                    place * seconds : (place + 1) * seconds
                ]


def finish(z, core, mine, other, units, width, model):
    return pl.pallas_call(
        finish_kernel,
        out_shape=(
            jax.ShapeDtypeStruct((units, width), F32),
            jax.ShapeDtypeStruct((width, model), F32),
        ),
        in_specs=[SM, VM, VM],
        out_specs=(VM, VM),
        compiler_params=params(),
    )(jnp.stack([z, core]), mine, other)


def forward_kernel(packed_ref, weight_ref, out_ref):
    out_ref[...] = dot_nt(packed_ref[...], weight_ref[...]).astype(BF16)


def forward(packed, weight):
    (slots, units), model = packed.shape, weight.shape[0]
    tile = 1024
    return pl.pallas_call(
        forward_kernel,
        grid=(model // tile,),
        out_shape=jax.ShapeDtypeStruct((slots, model), BF16),
        in_specs=[
            pl.BlockSpec((slots, units), lambda i: (0, 0)),
            pl.BlockSpec((tile, units), lambda i: (i, 0)),
        ],
        out_specs=pl.BlockSpec((slots, tile), lambda i: (0, i)),
        compiler_params=params(WHOLE_VMEM),
        cost_estimate=pl.CostEstimate(
            flops=2 * slots * units * model,
            bytes_accessed=2 * (slots * units + units * model + slots * model),
            transcendentals=0,
        ),
    )(packed, weight)


def backward_kernel(cot_ref, inner_ref, weight_ref, first_ref, out_ref):
    total = dot_nn(cot_ref[...], weight_ref[...]) + dot_nt(inner_ref[...], first_ref[...])
    out_ref[...] = total.astype(BF16)


def backward(cotangent, inner_gradient, weight, first_factors):
    (slots, model), units = cotangent.shape, weight.shape[1]
    tile = 896
    return pl.pallas_call(
        backward_kernel,
        grid=(units // tile,),
        out_shape=jax.ShapeDtypeStruct((slots, units), BF16),
        in_specs=[
            pl.BlockSpec((slots, model), lambda i: (0, 0)),
            pl.BlockSpec((slots, LANES), lambda i: (0, 0)),
            pl.BlockSpec((model, tile), lambda i: (0, i)),
            pl.BlockSpec((tile, LANES), lambda i: (i, 0)),
        ],
        out_specs=pl.BlockSpec((slots, tile), lambda i: (0, i)),
        compiler_params=params(WHOLE_VMEM),
        cost_estimate=pl.CostEstimate(
            flops=2 * slots * units * model,
            bytes_accessed=2 * (slots * units + units * model + slots * model),
            transcendentals=0,
        ),
    )(cotangent, inner_gradient, weight, first_factors)


def on_device(hidden, destination, job_per_tile, down_matrix, first_factors, second_factors, cotangent):
    rows, units = hidden.shape
    shard = rows // NZ
    width, model = second_factors.shape
    core = lax.rem(lax.axis_index("dp"), 2)
    z = lax.axis_index("tensor")

    weight = lax.all_gather(down_matrix.T, "dp", axis=0, tiled=True)
    sent = sort_rows(destination, hidden)
    got = lax.all_to_all(
        sent, "dp", split_axis=0, concat_axis=0, axis_index_groups=SAME_CORE, tiled=True
    )
    piece = widen_cotangent(z, job_per_tile, cotangent, second_factors)
    steps = gather_near(piece)
    got = after(got, *steps[1])

    packed = pack_rows(core, got, swap_core(got))
    slot_job = jnp.repeat(job_per_tile, rows // job_per_tile.shape[0], total_repeat_length=rows)
    column = jnp.arange(width, dtype=jnp.int32)
    column_job = column // ADAPTER_RANK
    inner_part = jnp.where(
        slot_job[:, None] == column_job[None, :], dot_nn(packed, first_factors), 0.0
    ).astype(BF16)
    fold = (column[None, :] % ADAPTER_RANK == jnp.arange(ADAPTER_RANK)[:, None]).astype(BF16)
    inner_part = dot_nt(fold, inner_part)
    inner_sum = sum_z(inner_part).astype(BF16)
    full_cotangent, inner_gradient = gather_far(piece, steps, after(steps[-1], inner_part), z)
    inner = jnp.where(
        slot_job[None, :] == column_job[:, None], jnp.tile(inner_sum, (width // ADAPTER_RANK, 1)), 0
    ).astype(BF16)
    my_slots = (
        jnp.arange(rows, dtype=jnp.int32)[:, None]
        == z * shard + jnp.arange(shard, dtype=jnp.int32)[None, :]
    ).astype(BF16)
    my_inner = lax.dot_general(
        my_slots, inner, (((0,), (1,)), ((), ())), preferred_element_type=F32
    ).astype(BF16)

    first_part = dot_tn(packed, inner_gradient).astype(BF16)
    sums = shares(z, inner, full_cotangent, first_part)
    parts = lax.all_to_all(sums, "dp", split_axis=0, concat_axis=0, tiled=True)
    share = jnp.sum(parts.astype(F32), axis=0).astype(BF16)
    firsts = units // (2 * CHIPS)
    share = jnp.concatenate([share[:firsts], gather_xor(share[firsts:])], axis=0)
    spread = jnp.broadcast_to(share[None], (CHIPS,) + share.shape)
    every = lax.all_to_all(
        spread, "dp", split_axis=0, concat_axis=0, axis_index_groups=SAME_CORE, tiled=True
    )

    weight = after(weight, sums)
    base = after(forward(packed, weight), parts)
    summed = lax.psum_scatter(base, "tensor", scatter_dimension=0, tiled=True)
    hidden_gradient = backward(full_cotangent, inner_gradient, weight, first_factors)
    every = after(every, hidden_gradient)
    grad_a, second_gradient = finish(z, core, every, swap_core(every), units, width, model)
    adapted = lax.optimization_barrier(ADAPTER_SCALE * dot_nn(my_inner, second_factors))
    mixed = (summed.astype(F32) + adapted).astype(BF16)
    return (mixed, hidden_gradient, grad_a, second_gradient)


def solution(mesh):
    return jax.shard_map(
        on_device,
        mesh=mesh,
        in_specs=(
            P("dp", "tensor"),
            P("dp"),
            P("dp"),
            P("tensor", "dp"),
            P("tensor", None),
            P(),
            P(("dp", "tensor"), None),
        ),
        out_specs=(P(("dp", "tensor"), None), P("dp", "tensor"), P("tensor", None), P()),
        check_vma=False,
    )
```

```python
import functools

import jax
import jax.numpy as jnp
from jax import lax
from jax.experimental import pallas as pl
from jax.experimental.pallas import tpu as pltpu
from jax.sharding import PartitionSpec as P

ADAPTER_RANK = 16
ADAPTER_SCALE = 2.0
NX, NY, NZ = 4, 4, 8
CHIPS = NX * NY
LANES = 128
VMEM_LIMIT = 40 * 1024 * 1024
WHOLE_VMEM = 58 * 1024 * 1024
F32 = jnp.float32
BF16 = jnp.bfloat16

SAME_CORE = [[2 * chip + core for chip in range(CHIPS)] for core in range(2)]


def after(values, *others):
    return lax.optimization_barrier((values, others))[0]


def swap_core(value):
    return lax.ppermute(value, "dp", [(i, i ^ 1) for i in range(2 * CHIPS)])


def dot_nt(left, right):
    return lax.dot_general(left, right, (((1,), (1,)), ((), ())), preferred_element_type=F32)


def dot_nn(left, right):
    return jnp.dot(left, right, preferred_element_type=F32)


def dot_tn(left, right):
    return lax.dot_general(left, right, (((0,), (0,)), ((), ())), preferred_element_type=F32)


def params(limit=VMEM_LIMIT):
    return pltpu.CompilerParams(vmem_limit_bytes=limit)


VM = pl.BlockSpec(memory_space=pltpu.VMEM)
SM = pl.BlockSpec(memory_space=pltpu.SMEM)


def sort_kernel(dest_ref, hidden_ref, out_ref):
    rows, units = hidden_ref.shape
    capacity = rows // (2 * CHIPS)
    dest = dest_ref[...]
    live = dest >= 0
    dest_f = dest.astype(F32)
    group = jnp.where(live, jnp.floor((dest_f + 0.5) * (1.0 / rows)), -1.0)
    across = jnp.broadcast_to(group, (rows, rows))
    down = across.T
    sub = lax.broadcasted_iota(jnp.int32, (rows, rows), 0)
    lane = lax.broadcasted_iota(jnp.int32, (rows, rows), 1)
    earlier = jnp.where((across == down) & (sub < lane), 1.0, 0.0)
    position = jnp.sum(earlier, axis=0, keepdims=True)
    place = jnp.where(live, group * capacity + position, -1.0)
    pick = jnp.where(sub.astype(F32) == place, 1.0, 0.0).astype(BF16)
    for tile in range(units // 256):
        cols = slice(tile * 256, (tile + 1) * 256)
        out_ref[:, cols] = dot_nn(pick, hidden_ref[:, cols]).astype(BF16)
    chip = jnp.floor((dest_f + 0.5) * (1.0 / (2 * rows)))
    code = jnp.where(live, dest_f - chip * (2 * rows) + 1.0, 0.0)
    high = jnp.floor(code * (1.0 / 16.0))
    low = code - 16.0 * high
    row = lax.broadcasted_iota(jnp.int32, (LANES, rows), 0)
    codes = jnp.where(row == 0, high, jnp.where(row == 1, low, 0.0)).astype(BF16)
    out_ref[:, units:] = dot_nt(pick, codes).astype(BF16)


def sort_rows(destination, hidden):
    rows, units = hidden.shape
    return pl.pallas_call(
        sort_kernel,
        out_shape=jax.ShapeDtypeStruct((rows, units + LANES), BF16),
        in_specs=[VM, VM],
        out_specs=VM,
        compiler_params=params(),
    )(destination.reshape(1, rows), hidden)


def pack_kernel(core_ref, mine_ref, other_ref, out_ref):
    slots, units = out_ref.shape
    rows = mine_ref.shape[0]
    weight_row = lax.broadcasted_iota(jnp.int32, (8, LANES), 1)
    weight = jnp.where(weight_row == 0, 16.0, jnp.where(weight_row == 1, 1.0, 0.0)).astype(BF16)
    wanted = lax.broadcasted_iota(jnp.int32, (slots, rows), 0) + core_ref[0] * slots + 1
    wanted = wanted.astype(F32)
    picks = []
    for got in (mine_ref, other_ref):
        code = dot_nt(weight, got[:, units:])[0:1, :]
        picks.append(jnp.where(wanted == code, 1.0, 0.0).astype(BF16))
    for tile in range(units // 256):
        cols = slice(tile * 256, (tile + 1) * 256)
        out_ref[:, cols] = (
            dot_nn(picks[0], mine_ref[:, cols]) + dot_nn(picks[1], other_ref[:, cols])
        ).astype(BF16)


def pack_rows(core, mine, other):
    rows, wide = mine.shape
    return pl.pallas_call(
        pack_kernel,
        out_shape=jax.ShapeDtypeStruct((rows, wide - LANES), BF16),
        in_specs=[SM, VM, VM],
        out_specs=VM,
        compiler_params=params(),
    )(core.reshape(1), mine, other)


def cotangent_kernel(z_ref, jobs_ref, cot_ref, second_ref, out_ref):
    rows, model = cot_ref.shape
    inner = ADAPTER_SCALE * dot_nt(cot_ref[...], second_ref[...])
    width = inner.shape[1]
    slot = lax.broadcasted_iota(jnp.int32, (rows, width), 0) + z_ref[0] * rows
    tile = NZ * rows // 3
    job = jnp.where(slot < tile, jobs_ref[0], jnp.where(slot < 2 * tile, jobs_ref[1], jobs_ref[2]))
    column = lax.broadcasted_iota(jnp.int32, (rows, width), 1)
    first = job * ADAPTER_RANK
    chosen = (column >= first) & (column < first + ADAPTER_RANK)
    out_ref[:, :model] = cot_ref[...]
    out_ref[:, model:] = jnp.where(chosen, inner, 0.0).astype(BF16)


def widen_cotangent(z, jobs, cotangent, second):
    rows, model = cotangent.shape
    return pl.pallas_call(
        cotangent_kernel,
        out_shape=jax.ShapeDtypeStruct((rows, model + second.shape[0]), BF16),
        in_specs=[SM, SM, VM, VM],
        out_specs=VM,
        compiler_params=params(),
    )(z.reshape(1), jobs, cotangent, second)


def order_kernel(half, z_ref, *refs):
    pieces, (model_ref, inner_ref, sem) = refs[:-3], refs[-3:]
    model = model_ref.shape[2]
    copies = []

    def copy(source, out_ref, offset, start, size):
        spot = lax.rem(z_ref[0] + (offset + NZ), NZ)
        copies.append(
            pltpu.make_async_copy(
                source, out_ref.at[spot, :, pl.ds(start, size)], sem.at[len(copies)]
            )
        )
        copies[-1].start()

    for piece, offset in zip(pieces[:-2], range(1 - NZ // 2, NZ // 2)):
        copy(piece.at[:, pl.ds(0, model)], model_ref, offset, 0, model)
        copy(piece.at[:, pl.ds(model, LANES)], inner_ref, offset, 0, LANES)
    low, high = pieces[-2:]
    copy(low, model_ref, NZ // 2, 0, half)
    copy(high.at[:, pl.ds(0, model - half)], model_ref, NZ // 2, half, model - half)
    copy(high.at[:, pl.ds(model - half, LANES)], inner_ref, NZ // 2, 0, LANES)
    for started in copies:
        started.wait()


def send_z(value, step):
    return lax.ppermute(value, "tensor", [(i, (i + step) % NZ) for i in range(NZ)])


def gather_near(piece):
    steps, up, down = [], piece, piece
    for _ in range(1, NZ // 2):
        up, down = lax.optimization_barrier((send_z(up, 1), send_z(down, -1)))
        steps.append((up, down))
    return steps


def last_parts(last):
    up, down = last
    half = up.shape[1] // (2 * LANES) * LANES
    return lax.optimization_barrier((up[:, :half], down[:, half:]))


def gather_far(piece, steps, parts, z):
    rows, wide = piece.shape
    half = parts[0].shape[1]
    far = lax.optimization_barrier((send_z(parts[0], 1), send_z(parts[1], -1)))
    pieces = [up for up, _ in steps[::-1]] + [piece] + [down for _, down in steps] + list(far)
    anywhere = pl.BlockSpec(memory_space=pl.ANY)
    model, inner = pl.pallas_call(
        functools.partial(order_kernel, half),
        out_shape=(
            jax.ShapeDtypeStruct((NZ, rows, wide - LANES), BF16),
            jax.ShapeDtypeStruct((NZ, rows, LANES), BF16),
        ),
        in_specs=[SM] + [anywhere] * len(pieces),
        out_specs=(VM, VM),
        scratch_shapes=[pltpu.SemaphoreType.DMA((2 * NZ + 1,))],
        compiler_params=params(),
    )(z.reshape(1), *pieces)
    return model.reshape(NZ * rows, -1), inner.reshape(NZ * rows, LANES)


def sum_z(value, hold):
    step = 1
    while step < NZ:
        if 2 * step == NZ:
            value = after(value, *hold)
        value = value + lax.ppermute(value, "tensor", [(i, i ^ step) for i in range(NZ)])
        step *= 2
    return value


def gather_xor(value):
    step = 1
    while step < NZ:
        other = lax.ppermute(value, "tensor", [(i, i ^ step) for i in range(NZ)])
        value = jnp.concatenate([value, other], axis=0)
        step *= 2
    return value


def share_kernel(_, inner_ref, cot_ref, first_ref, out_ref):
    parts, rows, _ = out_ref.shape
    firsts = first_ref.shape[0] // parts
    seconds = rows - firsts
    block = (ADAPTER_SCALE * dot_nn(inner_ref[...], cot_ref[...])).astype(BF16)
    each = block.shape[0] // seconds
    for i in range(parts):
        out_ref[i, :firsts, :] = first_ref[i * firsts : (i + 1) * firsts, :]
        row, column = (i % each) * seconds, (i // each) * LANES
        out_ref[i, firsts:, :] = block[row : row + seconds, column : column + LANES]


def shares(z, inner, cotangent, first_part):
    parts = 2 * CHIPS
    rows = first_part.shape[0] // parts + inner.shape[0] * cotangent.shape[1] // (NZ * parts * LANES)
    slots, model = cotangent.shape
    return pl.pallas_call(
        share_kernel,
        out_shape=jax.ShapeDtypeStruct((parts, rows, LANES), BF16),
        grid_spec=pltpu.PrefetchScalarGridSpec(
            num_scalar_prefetch=1,
            grid=(1,),
            in_specs=[
                pl.BlockSpec(inner.shape, lambda i, z: (0, 0)),
                pl.BlockSpec((slots, model // NZ), lambda i, z: (0, z[0])),
                pl.BlockSpec(first_part.shape, lambda i, z: (0, 0)),
            ],
            out_specs=pl.BlockSpec((parts, rows, LANES), lambda i, z: (0, 0, 0)),
        ),
        compiler_params=params(WHOLE_VMEM),
    )(z.reshape(1), inner, cotangent, first_part)


def finish_kernel(place_ref, mine_ref, other_ref, first_ref, second_ref):
    chips, rows, _ = mine_ref.shape
    firsts = first_ref.shape[0] // (2 * chips)
    seconds = (rows - firsts) // NZ
    each = second_ref.shape[0] // seconds
    wide = second_ref.shape[1] // NZ
    for core, part_ref in ((place_ref[1], mine_ref), (1 - place_ref[1], other_ref)):
        for chip in range(chips):
            spot = pl.multiple_of((2 * chip + core) * firsts, 8)
            first_ref[pl.ds(spot, firsts), :] = part_ref[chip, :firsts, :].astype(F32)
            share = part_ref[chip, firsts:, :].astype(F32)
            row = pl.multiple_of(((2 * chip) % each + core) * seconds, 8)
            for place in range(NZ):
                column = (place_ref[0] ^ place) * wide + (2 * chip // each) * LANES
                second_ref[pl.ds(row, seconds), pl.ds(pl.multiple_of(column, LANES), LANES)] = share[
                    place * seconds : (place + 1) * seconds
                ]


def finish(z, core, mine, other, units, width, model):
    return pl.pallas_call(
        finish_kernel,
        out_shape=(
            jax.ShapeDtypeStruct((units, width), F32),
            jax.ShapeDtypeStruct((width, model), F32),
        ),
        in_specs=[SM, VM, VM],
        out_specs=(VM, VM),
        compiler_params=params(),
    )(jnp.stack([z, core]), mine, other)


def forward_kernel(packed_ref, weight_ref, out_ref):
    out_ref[...] = dot_nt(packed_ref[...], weight_ref[...]).astype(BF16)


def forward(packed, weight):
    (slots, units), model = packed.shape, weight.shape[0]
    tile = 1024
    return pl.pallas_call(
        forward_kernel,
        grid=(model // tile,),
        out_shape=jax.ShapeDtypeStruct((slots, model), BF16),
        in_specs=[
            pl.BlockSpec((slots, units), lambda i: (0, 0)),
            pl.BlockSpec((tile, units), lambda i: (i, 0)),
        ],
        out_specs=pl.BlockSpec((slots, tile), lambda i: (0, i)),
        compiler_params=params(WHOLE_VMEM),
        cost_estimate=pl.CostEstimate(
            flops=2 * slots * units * model,
            bytes_accessed=2 * (slots * units + units * model + slots * model),
            transcendentals=0,
        ),
    )(packed, weight)


def backward_kernel(cot_ref, inner_ref, weight_ref, first_ref, out_ref):
    total = dot_nn(cot_ref[...], weight_ref[...]) + dot_nt(inner_ref[...], first_ref[...])
    out_ref[...] = total.astype(BF16)


def backward(cotangent, inner_gradient, weight, first_factors):
    (slots, model), units = cotangent.shape, weight.shape[1]
    tile = 896
    return pl.pallas_call(
        backward_kernel,
        grid=(units // tile,),
        out_shape=jax.ShapeDtypeStruct((slots, units), BF16),
        in_specs=[
            pl.BlockSpec((slots, model), lambda i: (0, 0)),
            pl.BlockSpec((slots, LANES), lambda i: (0, 0)),
            pl.BlockSpec((model, tile), lambda i: (0, i)),
            pl.BlockSpec((tile, LANES), lambda i: (i, 0)),
        ],
        out_specs=pl.BlockSpec((slots, tile), lambda i: (0, i)),
        compiler_params=params(WHOLE_VMEM),
        cost_estimate=pl.CostEstimate(
            flops=2 * slots * units * model,
            bytes_accessed=2 * (slots * units + units * model + slots * model),
            transcendentals=0,
        ),
    )(cotangent, inner_gradient, weight, first_factors)


def on_device(hidden, destination, job_per_tile, down_matrix, first_factors, second_factors, cotangent):
    rows, units = hidden.shape
    shard = rows // NZ
    width, model = second_factors.shape
    core = lax.rem(lax.axis_index("dp"), 2)
    z = lax.axis_index("tensor")

    weight = lax.all_gather(down_matrix.T, "dp", axis=0, tiled=True)
    sent = sort_rows(destination, hidden)
    got = lax.all_to_all(
        sent, "dp", split_axis=0, concat_axis=0, axis_index_groups=SAME_CORE, tiled=True
    )
    piece = widen_cotangent(z, job_per_tile, cotangent, second_factors)
    steps = gather_near(piece)
    got = after(got, *steps[1])

    packed = pack_rows(core, got, swap_core(got))
    slot_job = jnp.repeat(job_per_tile, rows // job_per_tile.shape[0], total_repeat_length=rows)
    column = jnp.arange(width, dtype=jnp.int32)
    column_job = column // ADAPTER_RANK
    inner_part = jnp.where(
        slot_job[:, None] == column_job[None, :], dot_nn(packed, first_factors), 0.0
    ).astype(BF16)
    fold = (column[None, :] % ADAPTER_RANK == jnp.arange(ADAPTER_RANK)[:, None]).astype(BF16)
    inner_part = dot_nt(fold, inner_part)
    opposite = last_parts(after(steps[-1], inner_part))
    inner_sum = sum_z(inner_part, opposite).astype(BF16)
    full_cotangent, inner_gradient = gather_far(piece, steps, opposite, z)
    inner = jnp.where(
        slot_job[None, :] == column_job[:, None], jnp.tile(inner_sum, (width // ADAPTER_RANK, 1)), 0
    ).astype(BF16)
    my_slots = (
        jnp.arange(rows, dtype=jnp.int32)[:, None]
        == z * shard + jnp.arange(shard, dtype=jnp.int32)[None, :]
    ).astype(BF16)
    my_inner = lax.dot_general(
        my_slots, inner, (((0,), (1,)), ((), ())), preferred_element_type=F32
    ).astype(BF16)

    first_part = dot_tn(packed, inner_gradient).astype(BF16)
    sums = shares(z, inner, full_cotangent, first_part)
    parts = lax.all_to_all(sums, "dp", split_axis=0, concat_axis=0, tiled=True)
    share = jnp.sum(parts.astype(F32), axis=0).astype(BF16)
    firsts = units // (2 * CHIPS)
    share = jnp.concatenate([share[:firsts], gather_xor(share[firsts:])], axis=0)
    spread = jnp.broadcast_to(share[None], (CHIPS,) + share.shape)
    every = lax.all_to_all(
        spread, "dp", split_axis=0, concat_axis=0, axis_index_groups=SAME_CORE, tiled=True
    )

    weight = after(weight, sums)
    base = after(forward(packed, weight), parts)
    summed = lax.psum_scatter(base, "tensor", scatter_dimension=0, tiled=True)
    hidden_gradient = backward(full_cotangent, inner_gradient, weight, first_factors)
    every = after(every, hidden_gradient)
    grad_a, second_gradient = finish(z, core, every, swap_core(every), units, width, model)
    adapted = lax.optimization_barrier(ADAPTER_SCALE * dot_nn(my_inner, second_factors))
    mixed = (summed.astype(F32) + adapted).astype(BF16)
    return (mixed, hidden_gradient, grad_a, second_gradient)


def solution(mesh):
    return jax.shard_map(
        on_device,
        mesh=mesh,
        in_specs=(
            P("dp", "tensor"),
            P("dp"),
            P("dp"),
            P("tensor", "dp"),
            P("tensor", None),
            P(),
            P(("dp", "tensor"), None),
        ),
        out_specs=(P(("dp", "tensor"), None), P("dp", "tensor"), P("tensor", None), P()),
        check_vma=False,
    )
```
